128 devices in a mesh: owner: 16 (over z, y), kv: 8 (over x, core).
Axes of the slice: x: 4, y: 4, z: 4, core: 2. Of those that a mesh axis runs over, the one named last changes fastest.
Arguments:
- queries: bfloat16 [512, 8192], P('owner', 'kv'), may hold values from -4.5 to 4.5
- prefix_cache: bfloat16 [16, 8192, 8, 256], P('owner', None, 'kv'), may hold values from -8 to 8
- suffix_cache: bfloat16 [512, 1024, 8, 256], P('owner', None, 'kv'), may hold values from -8 to 8
- suffix_len: int32 [512], P('owner'), may hold values from 1 to 1024, 393216 in all
- fork_prefix: int32 [512, 1], P('owner'), may hold values from 0 to 15; in each aligned block of 32 rows (0 to 31, 32 to 63, ...) at most 4 rows name the same one
- prefix_slot: int32 [16], replicated, may hold values from 0 to 15, each once
- out_weight: bfloat16 [8192, 8192], P('kv', 'owner'), may hold values from -0.375 to 0.375
Outputs:
- projected: bfloat16 [512, 8192], P('kv', 'owner')
The draws below stay inside these ranges and needn't reach their ends.
Inputs may be any that keep to these rules, and one draw needn't show every extreme that they name: `fork_prefix`: within the 32 rows of one owner index no prefix id appears more than 4 times, and on some owner index one appears exactly 4 times; every prefix id appears on some row. `prefix_slot`: each stored row is named by exactly one prefix id.
All inputs are finite; a program needn't handle non-finite values. No bound on the sum of `suffix_len` on one device may be relied on, other than what follows from the above.
Results may differ from the reference program's by a relative error of at most 0.019.
Values may be sent and summed in bfloat16 or wider, within the bound.
No kernel may reach another device: no remote copies, remote signals or barrier semaphores. Data moves between devices by JAX's collectives and lax.ppermute only.
A program may use at most 192 MiB of HBM per device.

```python
import math
import jax
import jax.numpy as jnp
import numpy as np
from jax import lax

D = 8192
HEADS = 64
KVH = 8
HD = 128
ROWS_DEV = 32
LP = 8192
S_MAX = 1024
GROUP = 8
PREFIXES = 16
ROWS = 512
CAP = 4


def draw_queries(key, part):
    key = jax.random.fold_in(key, 7)
    shape = (ROWS, HEADS * HD)
    return jnp.clip(jax.random.normal(key, shape, jnp.float32), -4.5, 4.5).astype(jnp.bfloat16)


def draw_prefix_cache(key, part):
    key = jax.random.fold_in(key, 3)
    shape = (PREFIXES, LP, KVH, 2 * HD)
    return jnp.clip(2.0 * jax.random.normal(key, shape, jnp.float32), -8.0, 8.0).astype(jnp.bfloat16)


def draw_suffix_cache(key, part):
    key = jax.random.fold_in(key, 5)
    shape = (ROWS, S_MAX, KVH, 2 * HD)
    return jnp.clip(2.0 * jax.random.normal(key, shape, jnp.float32), -8.0, 8.0).astype(jnp.bfloat16)


def level_of(key, dims, split, low, top_value):
    factor_of = 1.0
    for dim, blocks in split:
        draws = jax.random.uniform(jax.random.fold_in(jax.random.fold_in(key, 6), dim), (blocks,), jnp.float32, low / len(split), top_value / len(split))
        factor_of = factor_of * jnp.repeat(jnp.exp(draws), dims[dim] // blocks).reshape((-1,) + (1,) * (len(dims) - 1 - dim))
    return factor_of


def profile(amount, total, reach, slope):
    portions = [(1 << 20) // math.isqrt(grade ** slope) + 1 for grade in range(2, amount + 1)]
    surplus, counts = total - reach - (amount - 1), [1] * (amount - 1)
    while surplus > 0:
        candidates = [i for i in range(amount - 1) if counts[i] < reach]
        mass, left = sum([portions[i] for i in candidates]), surplus
        for i in candidates:
            more = min(reach - counts[i], max(1, left * portions[i] // mass), surplus)
            counts[i] = counts[i] + more
            surplus = surplus - more
    return np.array([reach] + counts)


def ragged_sizes(rng, number_of, total, reach, skew):
    if number_of == 2:
        one = jax.random.randint(rng, (), max(1, total - reach), min(reach, total - 1) + 1)
        return jnp.stack([one, total - one])
    tallies = jnp.asarray(profile(number_of, total, reach, skew), jnp.int32)
    pairs = (number_of - 1) // 2
    donor, taker = tallies[1:1 + 2 * pairs:2], tallies[2:2 + 2 * pairs:2]
    slack = jnp.minimum(donor - 1, reach - taker)
    passed = jax.random.randint(jax.random.fold_in(rng, 1), (pairs,), 0, 1 << 20) % (slack + 1)
    tallies = tallies.at[1:1 + 2 * pairs:2].set(donor - passed).at[2:2 + 2 * pairs:2].set(taker + passed)
    return tallies[jax.random.permutation(jax.random.fold_in(rng, 2), number_of)]


def deal_out(key, own, number, rows, number_of, top, most, skew):
    sequence = jax.random.permutation(key, number_of)
    packed, common = load_shares(number_of, rows * top, most, skew, True), load_shares(number_of, rows * top, most, skew, False)
    places = jnp.arange(number_of)

    def named(sizes, turn):
        used = int((sizes > 0).sum())
        fixed = max(1, used // 4)
        passed = fixed + (places - fixed + turn * (used - fixed)) % max(1, number_of - fixed)
        return jnp.zeros((number_of,), jnp.int32).at[sequence[jnp.where(places < fixed, places, passed)]].set(jnp.asarray(sizes, jnp.int32))

    sizes = jnp.where(number % 4 == 0, named(packed, number // 4), named(common, number - number // 4 - 1))
    mixed = jax.random.permutation(jax.random.fold_in(own, 3), number_of)
    giver, sink = mixed[0:number_of // 2 * 2:2], mixed[1:number_of // 2 * 2:2]
    margin = jnp.minimum(sizes[giver] - 1, most - sizes[sink]) // 2
    margin = jnp.where((giver == sequence[0]) | (sink == sequence[0]) | (sizes[sink] == 0), 0, jnp.maximum(margin, 0))
    passed = jax.random.randint(jax.random.fold_in(own, 4), (number_of // 2,), 0, 1 << 20) % (margin + 1)
    sizes = sizes.at[giver].add(-passed).at[sink].add(passed)
    members = jnp.searchsorted(jnp.cumsum(sizes), jnp.arange(rows * top), side="right").astype(jnp.int32)
    grid = members.reshape(top, rows).T
    grid = grid[jax.random.permutation(jax.random.fold_in(own, 1), rows)]
    turn = jax.random.randint(jax.random.fold_in(own, 2), (rows, 1), 0, top)
    return jnp.take_along_axis(grid, (jnp.arange(top)[None, :] + turn) % top, axis=1)


def load_shares(number_of, total, reach, slope, full):
    loads = [(1 << 20) // math.isqrt(standing ** slope) + 1 for standing in range(1, number_of + 1)]
    largest = reach if full else min(reach, max(-(-total // number_of), total * loads[0] // sum(loads)))
    least = 1 if total - largest >= number_of - 1 else 0
    given, rest = [largest] + [least] * (number_of - 1), total - largest - least * (number_of - 1)
    while rest > 0:
        candidates = [i for i in range(1, number_of) if given[i] < largest] or [i for i in range(1, number_of) if given[i] < reach]
        mass, remaining = sum([loads[i] for i in candidates]), rest
        for i in candidates:
            extra = min(reach - given[i], max(1, remaining * loads[i] // mass), rest)
            given[i] = given[i] + extra
            rest = rest - extra
    return np.array(given)


def bell_draw(key, dims, spread, reach, split=(), held_as=jnp.bfloat16):
    loudness = level_of(key, dims, split, -0.22, 0.18) if split else 1.0
    entries = jax.random.normal(key, dims, jnp.float32) * spread * loudness
    return jnp.minimum(jnp.maximum(entries, -reach), reach).astype(held_as)


def setup_inputs(seed: int = 0) -> dict:
    key_list = jax.random.split(jax.random.key(seed), 8)
    queries = draw_queries(jax.random.fold_in(key_list[7], 71), 0)
    prefix_cache = draw_prefix_cache(jax.random.fold_in(key_list[7], 71), 0)
    suffix_cache = draw_suffix_cache(jax.random.fold_in(key_list[7], 71), 0)
    suffix_len = ragged_sizes(key_list[3], ROWS, ROWS * S_MAX * 3 // 4, S_MAX, 1).astype(jnp.int32)
    fork_prefix_keys = jax.random.split(jax.random.fold_in(key_list[4], 1), ROWS // ROWS_DEV)
    fork_prefix_turns = jax.random.permutation(jax.random.fold_in(key_list[4], 3), ROWS // ROWS_DEV)
    fork_prefix = jax.vmap(lambda own, number: deal_out(jax.random.fold_in(key_list[4], 2), own, number, ROWS_DEV, PREFIXES, 1, CAP, 2))(fork_prefix_keys, fork_prefix_turns).reshape((ROWS, 1))
    prefix_slot = jax.random.permutation(key_list[5], PREFIXES).astype(jnp.int32)
    out_weight = bell_draw(key_list[6], (HEADS * HD, D), (HEADS * HD // 32) ** -0.5, 0.375, ((0, 8), (1, 16)))
    return {"queries": queries, "prefix_cache": prefix_cache, "suffix_cache": suffix_cache, "suffix_len": suffix_len, "fork_prefix": fork_prefix, "prefix_slot": prefix_slot, "out_weight": out_weight}


def row_attention(query_row, slot_row, length_row, suffix_row, prefix_cache):
    score_scale = HD ** -0.5
    cached = lax.dynamic_index_in_dim(prefix_cache, slot_row, 0, keepdims=False)
    query_f = query_row.reshape(KVH, GROUP, HD).astype(jnp.float32)
    scores_pre = jnp.einsum("gjd,kgd->gjk", query_f, cached[:, :, :HD].astype(jnp.float32)) * score_scale
    top_pre = jnp.max(scores_pre, axis=-1)
    weights_pre = jnp.exp(scores_pre - top_pre[..., None])
    total_pre = jnp.sum(weights_pre, axis=-1)
    rounded_pre = lax.optimization_barrier(weights_pre.astype(jnp.bfloat16)).astype(jnp.float32)
    summed_pre = jnp.einsum("gjk,kgd->gjd", rounded_pre, cached[:, :, HD:].astype(jnp.float32))
    scores_suf = jnp.einsum("gjd,sgd->gjs", query_f, suffix_row[:, :, :HD].astype(jnp.float32)) * score_scale
    live_mask = (jnp.arange(S_MAX, dtype=jnp.int32) < length_row)[None, None, :]
    masked = jnp.where(live_mask, scores_suf, jnp.float32(-1e30))
    top_suf = jnp.max(masked, axis=-1)
    weights_suf = jnp.where(live_mask, jnp.exp(masked - top_suf[..., None]), jnp.float32(0.0))
    total_suf = jnp.sum(weights_suf, axis=-1)
    rounded_suf = lax.optimization_barrier(weights_suf.astype(jnp.bfloat16)).astype(jnp.float32)
    summed_suf = jnp.einsum("gjs,sgd->gjd", rounded_suf, suffix_row[:, :, HD:].astype(jnp.float32))
    top_all = jnp.maximum(top_pre, top_suf)
    factor_pre = jnp.exp(top_pre - top_all)
    factor_suf = jnp.exp(top_suf - top_all)
    numerator = summed_pre * factor_pre[..., None] + summed_suf * factor_suf[..., None]
    denominator = total_pre * factor_pre + total_suf * factor_suf
    return (numerator / denominator[..., None]).reshape(HEADS * HD).astype(jnp.bfloat16)


def reference(queries, prefix_cache, suffix_cache, suffix_len, fork_prefix, prefix_slot, out_weight):
    row_slots = jnp.take(prefix_slot, fork_prefix[:, 0], axis=0).astype(jnp.int32)

    def one_row(row_items):
        return row_attention(row_items[0], row_items[1], row_items[2], row_items[3], prefix_cache)

    attended = lax.map(one_row, (queries, row_slots, suffix_len.astype(jnp.int32), suffix_cache))
    return jnp.dot(attended, out_weight, preferred_element_type=jnp.float32).astype(jnp.bfloat16)
```

```python
import functools

import jax
import jax.numpy as jnp
from jax import lax
from jax.experimental import pallas as pl
from jax.experimental.pallas import tpu as pltpu
from jax.sharding import PartitionSpec as P

LOG2E = 1.4426950408889634
NT = (((1,), (1,)), ((), ()))
VMEM = pl.BlockSpec(memory_space=pltpu.VMEM)
SMEM = pl.BlockSpec(memory_space=pltpu.SMEM)
ANY = pl.BlockSpec(memory_space=pl.ANY)
MIB = 2**20


def one_hot_slots(fork_ref, slot_ref, capacity):
    rows = fork_ref.shape[1]
    prefixes = slot_ref.shape[1]
    sub = lax.broadcasted_iota(jnp.int32, (rows, rows), 0)
    lane = lax.broadcasted_iota(jnp.int32, (rows, rows), 1)
    eye = sub == lane
    fork_row = jnp.broadcast_to(fork_ref[...], (rows, rows))
    fork_col = jnp.sum(jnp.where(eye, fork_row, 0), axis=1, keepdims=True)
    picked = fork_col == lax.broadcasted_iota(jnp.int32, (rows, prefixes), 1)
    slots_all = jnp.broadcast_to(slot_ref[...], (rows, prefixes))
    stored_col = jnp.sum(jnp.where(picked, slots_all, 0), axis=1, keepdims=True)
    stored_row = jnp.sum(
        jnp.where(eye, jnp.broadcast_to(stored_col, (rows, rows)), 0), axis=0, keepdims=True
    )
    earlier = (stored_col == stored_row) & (sub < lane)
    rank_row = jnp.sum(earlier.astype(jnp.int32), axis=0, keepdims=True)
    target = stored_row * capacity + rank_row
    count = prefixes * capacity
    return lax.broadcasted_iota(jnp.int32, (count, rows), 0) == target


def route_kernel(fork_ref, slot_ref, query_ref, out_ref, *, capacity):
    hot = one_hot_slots(fork_ref, slot_ref, capacity).astype(jnp.bfloat16)
    out_ref[...] = jnp.dot(hot, query_ref[...], preferred_element_type=jnp.float32).astype(
        jnp.bfloat16
    )


def suffix_kernel(len_ref, q_ref, kv_hbm, out_ref, lse_ref, kv, sems, q_s, o_s, *, group, scale):
    rows, keys, width = kv.shape
    hd = width // 2
    heads = q_ref.shape[1] // hd
    c2 = scale * LOG2E

    def copy_of(r):
        return pltpu.make_async_copy(kv_hbm.at[r], kv.at[r], sems.at[r])

    def issue(r, carry):
        copy_of(r).start()
        return carry

    lax.fori_loop(0, rows, issue, 0)
    for h in range(heads):
        q_s[pl.ds(h, rows, stride=heads), :] = q_ref[:, h * hd : (h + 1) * hd].astype(jnp.float32)
    span = group * heads

    def step(g, carry):
        def wait(i, c):
            copy_of(g * group + i).wait()
            return c

        lax.fori_loop(0, group, wait, 0)
        row_id = lax.broadcasted_iota(jnp.int32, (span, 1), 0) // heads
        length = jnp.zeros((span, 1), jnp.int32)
        for i in range(group):
            length = jnp.where(row_id == i, len_ref[g * group + i], length)
        base = pl.multiple_of(g * span, span)
        s = jnp.concatenate(
            [
                lax.dot_general(
                    q_s[pl.ds(base + i * heads, heads), :].astype(jnp.bfloat16),
                    kv[g * group + i, :, :hd],
                    NT,
                    preferred_element_type=jnp.float32,
                )
                for i in range(group)
            ],
            axis=0,
        )
        live = lax.broadcasted_iota(jnp.int32, (span, keys), 1) < length
        s = jnp.where(live, s, -1e30)
        m = jnp.max(s, axis=-1, keepdims=True)
        p = jnp.where(live, jnp.exp2((s - m) * c2), 0.0)
        total = jnp.sum(p, axis=-1, keepdims=True)
        o = jnp.concatenate(
            [
                jnp.dot(
                    p[i * heads : (i + 1) * heads].astype(jnp.bfloat16),
                    kv[g * group + i, :, hd:],
                    preferred_element_type=jnp.float32,
                )
                for i in range(group)
            ],
            axis=0,
        )
        o_s[pl.ds(base, span), :] = o / total
        lse_ref[pl.ds(base, span), :] = jnp.broadcast_to(m * c2 + jnp.log2(total), (span, hd))
        return carry

    lax.fori_loop(0, rows // group, step, 0)
    for h in range(heads):
        out_ref[:, h * hd : (h + 1) * hd] = o_s[pl.ds(h, rows, stride=heads), :]


def prefix_kernel(x_ref, kv_hbm, out_ref, kv, sems, q_s, m_s, acc_s, vt_s, *, kb, ct, scale, ahead):
    keys = kv.shape[0]
    hd = kv.shape[1] // 2
    slots = x_ref.shape[0]
    feat = x_ref.shape[1]
    heads = feat // hd
    n = keys // kb
    count = slots * heads
    c2 = scale * LOG2E

    def copy_of(c):
        part = pl.ds(c * kb, kb)
        return pltpu.make_async_copy(kv_hbm.at[part], kv.at[part], sems.at[c])

    for c in range(min(ahead, n)):
        copy_of(c).start()
    qf = jnp.concatenate([x_ref[:, h * hd : (h + 1) * hd] for h in range(heads)], axis=0)
    qf = qf.astype(jnp.float32).T * c2
    hi = qf.astype(jnp.bfloat16)
    q_s[:hd, :] = hi
    q_s[hd:, :] = (qf - hi.astype(jnp.float32)).astype(jnp.bfloat16)
    vt_s[hd:, :] = jnp.ones((vt_s.shape[0] - hd, kb), jnp.bfloat16)

    def scores(c, t):
        k = kv[c * kb : (c + 1) * kb, :hd]
        return jnp.dot(
            jnp.concatenate([k, k], axis=1),
            q_s[:, t * ct : (t + 1) * ct],
            preferred_element_type=jnp.float32,
        )

    items = [(c, t) for c in range(n) for t in range(count // ct)]
    copy_of(0).wait()
    s_next = scores(*items[0])
    for idx, (c, t) in enumerate(items):
        s = s_next
        if idx + 1 < len(items):
            c1, t1 = items[idx + 1]
            if t1 == 0:
                copy_of(c1).wait()
                if c1 + ahead - 1 < n:
                    copy_of(c1 + ahead - 1).start()
            s_next = scores(c1, t1)
        if t == 0:
            vt_s[:hd, :] = kv[c * kb : (c + 1) * kb, hd:].T
        cols = slice(t * ct, (t + 1) * ct)
        m_new = jnp.max(s, axis=0, keepdims=True)
        if c > 0:
            m_old = m_s[:1, cols]
            m_new = jnp.maximum(m_old, m_new)
        p = jnp.exp2(s - m_new)
        o = jnp.dot(vt_s[...], p.astype(jnp.bfloat16), preferred_element_type=jnp.float32)
        if c > 0:
            o = o + jnp.exp2(m_old - m_new) * acc_s[:, cols]
        m_s[:, cols] = jnp.broadcast_to(m_new, (8, ct))
        acc_s[:, cols] = o
    total = acc_s[hd : hd + 1, :]
    out = (acc_s[:hd, :] / total).T.astype(jnp.bfloat16)
    lse = jnp.broadcast_to(m_s[:1, :] + jnp.log2(total), (hd, count)).T
    lane = lax.broadcasted_iota(jnp.int32, (slots, hd), 1)
    pieces = jnp.zeros((slots, hd), jnp.float32)
    for h in range(heads):
        out_ref[:, h * hd : (h + 1) * hd] = out[h * slots : (h + 1) * slots, :]
        rest = lse[h * slots : (h + 1) * slots, :]
        for j in range(3):
            part = rest.astype(jnp.bfloat16).astype(jnp.float32)
            rest = rest - part
            pieces = jnp.where(lane == j * heads + h, part, pieces)
    out_ref[:, feat:] = pieces.astype(jnp.bfloat16)


def combine_kernel(fork_ref, slot_ref, recv_ref, osuf_ref, lsuf_ref, out_ref, *, capacity, heads):
    rows, feat = osuf_ref.shape
    hd = feat // heads
    copies = out_ref.shape[0]
    hot = one_hot_slots(fork_ref, slot_ref, capacity).astype(jnp.float32).T.astype(jnp.bfloat16)
    got = jnp.dot(hot, recv_ref[...], preferred_element_type=jnp.float32)
    for h in range(heads):
        cols = slice(h * hd, (h + 1) * hd)
        lse_pre = (
            got[:, feat + h : feat + h + 1]
            + got[:, feat + heads + h : feat + heads + h + 1]
            + got[:, feat + 2 * heads + h : feat + 2 * heads + h + 1]
        )
        lse_pre = jnp.broadcast_to(lse_pre, (rows, hd))
        lse_suf = lsuf_ref[pl.ds(h, rows, stride=heads), :]
        top = jnp.maximum(lse_pre, lse_suf)
        a = jnp.exp2(lse_pre - top)
        b = jnp.exp2(lse_suf - top)
        value = ((a * got[:, cols] + b * osuf_ref[:, cols]) / (a + b)).astype(jnp.bfloat16)
        for i in range(copies):
            out_ref[i, :, cols] = value


def body(queries, prefix_cache, suffix_cache, suffix_len, fork_prefix, prefix_slot, out_weight):
    rows, feat = queries.shape
    keys = prefix_cache.shape[1]
    hd = prefix_cache.shape[3] // 2
    heads = feat // hd
    owners = lax.axis_size("owner")
    prefixes = prefix_slot.shape[0]
    capacity = max(2, 2 * rows // prefixes)
    slots = prefixes * capacity
    scale = hd**-0.5
    fork_row = fork_prefix.reshape(1, rows)
    slot_row = prefix_slot.reshape(1, prefixes)
    limit = pltpu.CompilerParams(vmem_limit_bytes=56 * MIB)

    outgoing = pl.pallas_call(
        functools.partial(route_kernel, capacity=capacity),
        out_shape=jax.ShapeDtypeStruct((slots, feat), jnp.bfloat16),
        in_specs=[VMEM, VMEM, VMEM],
        out_specs=VMEM,
        name="route",
    )(fork_row, slot_row, queries)
    received = lax.all_to_all(
        outgoing.reshape(owners, capacity, feat), "owner", split_axis=0, concat_axis=0, tiled=True
    )

    suffix_keys = suffix_cache.shape[1]
    o_suf, lse_suf = pl.pallas_call(
        functools.partial(suffix_kernel, group=8, scale=scale),
        out_shape=(
            jax.ShapeDtypeStruct((rows, feat), jnp.float32),
            jax.ShapeDtypeStruct((rows * heads, hd), jnp.float32),
        ),
        in_specs=[SMEM, VMEM, ANY],
        out_specs=(VMEM, VMEM),
        scratch_shapes=[
            pltpu.VMEM((rows, suffix_keys, 2 * hd), jnp.bfloat16),
            pltpu.SemaphoreType.DMA((rows,)),
            pltpu.VMEM((rows * heads, hd), jnp.float32),
            pltpu.VMEM((rows * heads, hd), jnp.float32),
        ],
        compiler_params=limit,
        cost_estimate=pl.CostEstimate(
            flops=4 * rows * heads * suffix_keys * hd,
            bytes_accessed=rows * suffix_keys * 4 * hd,
            transcendentals=rows * heads * suffix_keys,
        ),
        name="suffix",
    )(suffix_len, queries, suffix_cache.reshape(rows, suffix_keys, 2 * hd))

    kb, ct = 2048, 256
    count = slots * heads
    partial = pl.pallas_call(
        functools.partial(prefix_kernel, kb=kb, ct=ct, scale=scale, ahead=3),
        out_shape=jax.ShapeDtypeStruct((slots, feat + hd), jnp.bfloat16),
        in_specs=[VMEM, ANY],
        out_specs=VMEM,
        scratch_shapes=[
            pltpu.VMEM((keys, 2 * hd), jnp.bfloat16),
            pltpu.SemaphoreType.DMA((keys // kb,)),
            pltpu.VMEM((2 * hd, count), jnp.bfloat16),
            pltpu.VMEM((8, count), jnp.float32),
            pltpu.VMEM((hd + 16, count), jnp.float32),
            pltpu.VMEM((hd + 16, kb), jnp.bfloat16),
        ],
        compiler_params=limit,
        cost_estimate=pl.CostEstimate(
            flops=4 * count * keys * hd,
            bytes_accessed=keys * 4 * hd,
            transcendentals=count * keys,
        ),
        name="prefix",
    )(received.reshape(slots, feat), prefix_cache.reshape(keys, 2 * hd))
    returned = lax.all_to_all(
        partial.reshape(owners, capacity, feat + hd),
        "owner",
        split_axis=0,
        concat_axis=0,
        tiled=True,
    )

    attended = pl.pallas_call(
        functools.partial(combine_kernel, capacity=capacity, heads=heads),
        out_shape=jax.ShapeDtypeStruct((owners, rows, feat), jnp.bfloat16),
        in_specs=[VMEM] * 5,
        out_specs=VMEM,
        name="combine",
    )(fork_row, slot_row, returned.reshape(slots, feat + hd), o_suf, lse_suf)
    gathered = lax.all_to_all(attended, "owner", split_axis=0, concat_axis=0, tiled=True)

    members = lax.axis_size("kv")
    chips = members // 2
    place = lax.axis_index("kv")
    chip, core = place // 2, place % 2
    block = owners * rows // members
    cols = out_weight.shape[1]
    full = gathered.reshape(chips, 2, block, feat)
    theirs = jnp.dot(
        lax.dynamic_index_in_dim(full, 1 - core, 1, keepdims=False).reshape(chips * block, feat),
        out_weight,
        preferred_element_type=jnp.float32,
    ).astype(jnp.bfloat16)
    from_pair = lax.ppermute(theirs, "kv", [(i, i ^ 1) for i in range(members)])
    mine = jnp.dot(
        lax.dynamic_index_in_dim(full, core, 1, keepdims=False).reshape(chips * block, feat),
        out_weight,
        preferred_element_type=jnp.float32,
    )
    pair_sum = (mine + from_pair.astype(jnp.float32)).reshape(chips, block, cols)
    pair_sent = pair_sum.astype(jnp.bfloat16)
    total = lax.dynamic_index_in_dim(pair_sum, chip, 0, keepdims=False)
    for d in range(1, chips):
        piece = lax.dynamic_index_in_dim(pair_sent, (chip + d) % chips, 0, keepdims=False)
        moved = lax.ppermute(
            piece,
            "kv",
            [(x * 2 + c, ((x + d) % chips) * 2 + c) for x in range(chips) for c in range(2)],
        )
        total = total + moved.astype(jnp.float32)
    return total.astype(jnp.bfloat16)


def solution(mesh):
    placed = (
        P("owner", "kv"),
        P("owner", None, "kv", None),
        P("owner", None, "kv", None),
        P("owner"),
        P("owner", None),
        P(),
        P("kv", "owner"),
    )
    return jax.shard_map(
        body, mesh=mesh, in_specs=placed, out_specs=P("kv", "owner"), check_vma=False
    )
```

```python
import functools

import jax
import jax.numpy as jnp
from jax import lax
from jax.experimental import pallas as pl
from jax.experimental.pallas import tpu as pltpu
from jax.sharding import PartitionSpec as P

LOG2E = 1.4426950408889634
NT = (((1,), (1,)), ((), ()))
VMEM = pl.BlockSpec(memory_space=pltpu.VMEM)
SMEM = pl.BlockSpec(memory_space=pltpu.SMEM)
ANY = pl.BlockSpec(memory_space=pl.ANY)
MIB = 2**20
GROUP_ROWS = 4


def one_hot_slots(fork_ref, slot_ref, capacity):
    rows = fork_ref.shape[1]
    prefixes = slot_ref.shape[1]
    sub = lax.broadcasted_iota(jnp.int32, (rows, rows), 0)
    lane = lax.broadcasted_iota(jnp.int32, (rows, rows), 1)
    eye = sub == lane
    fork_row = jnp.broadcast_to(fork_ref[...], (rows, rows))
    fork_col = jnp.sum(jnp.where(eye, fork_row, 0), axis=1, keepdims=True)
    picked = fork_col == lax.broadcasted_iota(jnp.int32, (rows, prefixes), 1)
    slots_all = jnp.broadcast_to(slot_ref[...], (rows, prefixes))
    stored_col = jnp.sum(jnp.where(picked, slots_all, 0), axis=1, keepdims=True)
    stored_row = jnp.sum(
        jnp.where(eye, jnp.broadcast_to(stored_col, (rows, rows)), 0), axis=0, keepdims=True
    )
    earlier = (stored_col == stored_row) & (sub < lane)
    rank_row = jnp.sum(earlier.astype(jnp.int32), axis=0, keepdims=True)
    return stored_row, rank_row, prefixes


def half_slots(placed, capacity):
    stored_row, rank_row, prefixes = placed
    rows = stored_row.shape[1]
    place = lax.broadcasted_iota(jnp.int32, (prefixes * 2 * capacity, rows), 0)
    return [
        (place == (stored_row * 2 + half) * capacity + rank_row).astype(jnp.float32)
        for half in range(2)
    ]


def route_kernel(fork_ref, slot_ref, query_ref, out_ref, *, capacity):
    rows, feat = query_ref.shape
    hot = half_slots(one_hot_slots(fork_ref, slot_ref, capacity), capacity)
    for half in range(2):
        cols = slice(half * feat // 2, (half + 1) * feat // 2)
        part = jnp.dot(
            hot[half].astype(jnp.bfloat16), query_ref[:, cols], preferred_element_type=jnp.float32
        )
        if half == 0:
            total = part
        else:
            total = total + part
    out_ref[...] = total.astype(jnp.bfloat16)


def suffix_kernel(
    len_ref, q_ref, kv_hbm, out_ref, lse_ref, kv, sems, q_s, o_s, *, first, group, scale
):
    rows, keys, width = kv.shape
    hd = width // 2
    heads = q_ref.shape[1] // hd
    c2 = scale * LOG2E

    def copy_of(r):
        return pltpu.make_async_copy(kv_hbm.at[first + r], kv.at[r], sems.at[r])

    def issue(r, carry):
        copy_of(r).start()
        return carry

    lax.fori_loop(0, rows, issue, 0)
    for h in range(heads):
        q_s[pl.ds(h, rows, stride=heads), :] = q_ref[
            first : first + rows, h * hd : (h + 1) * hd
        ].astype(jnp.float32)
    span = group * heads

    def step(g, carry):
        def wait(i, c):
            copy_of(g * group + i).wait()
            return c

        lax.fori_loop(0, group, wait, 0)
        row_id = lax.broadcasted_iota(jnp.int32, (span, 1), 0) // heads
        length = jnp.zeros((span, 1), jnp.int32)
        for i in range(group):
            length = jnp.where(row_id == i, len_ref[first + g * group + i], length)
        base = pl.multiple_of(g * span, span)
        s = jnp.concatenate(
            [
                lax.dot_general(
                    q_s[pl.ds(base + i * heads, heads), :].astype(jnp.bfloat16),
                    kv[g * group + i, :, :hd],
                    NT,
                    preferred_element_type=jnp.float32,
                )
                for i in range(group)
            ],
            axis=0,
        )
        live = lax.broadcasted_iota(jnp.int32, (span, keys), 1) < length
        s = jnp.where(live, s, -1e30)
        m = jnp.max(s, axis=-1, keepdims=True)
        p = jnp.where(live, jnp.exp2((s - m) * c2), 0.0)
        total = jnp.sum(p, axis=-1, keepdims=True)
        o = jnp.concatenate(
            [
                jnp.dot(
                    p[i * heads : (i + 1) * heads].astype(jnp.bfloat16),
                    kv[g * group + i, :, hd:],
                    preferred_element_type=jnp.float32,
                )
                for i in range(group)
            ],
            axis=0,
        )
        o_s[pl.ds(base, span), :] = o / total
        lse_ref[pl.ds(base, span), :] = jnp.broadcast_to(m * c2 + jnp.log2(total), (span, hd))
        return carry

    lax.fori_loop(0, rows // group, step, 0)
    for h in range(heads):
        out_ref[:, h * hd : (h + 1) * hd] = o_s[pl.ds(h, rows, stride=heads), :]


def prefix_kernel(
    x_ref, kv, after_ref, out_ref, q_s, s_s, acc_s, vt_s, *, kb, ct, sub, scale
):
    keys = kv.shape[0]
    hd = kv.shape[1] // 2
    slots, feat = x_ref.shape
    heads = feat // hd
    count = slots * heads
    c2 = scale * LOG2E
    qf = jnp.concatenate([x_ref[:, h * hd : (h + 1) * hd] for h in range(heads)], axis=0)
    qf = qf.astype(jnp.float32).T * c2
    hi = qf.astype(jnp.bfloat16)
    q_s[:hd, :] = hi
    q_s[hd:, :] = (qf - hi.astype(jnp.float32)).astype(jnp.bfloat16)
    vt_s[:, hd:, :] = jnp.ones((2, vt_s.shape[1] - hd, kb), jnp.bfloat16)
    tiles = count // ct
    steps = kb // sub
    items = [(c, t) for c in range(keys // kb) for t in range(tiles)]

    def scores(idx, j, highest):
        c, t = items[idx]
        here = slice(c * kb + j * sub, c * kb + (j + 1) * sub)
        k = kv[here, :hd]
        s = jnp.dot(
            jnp.concatenate([k, k], axis=1),
            q_s[:, t * ct : (t + 1) * ct],
            preferred_element_type=jnp.float32,
        )
        s_s[idx % 2, j * sub : (j + 1) * sub, :] = s
        if t == 0:
            vt_s[c % 2, :hd, j * sub : (j + 1) * sub] = kv[here, hd:].T
        top = jnp.max(s.reshape(sub // 8, 8, ct), axis=0)
        return top if highest is None else jnp.maximum(highest, top)

    highest = None
    for j in range(steps):
        highest = scores(0, j, highest)
    m_old = {}
    for idx, (c, t) in enumerate(items):
        cols = slice(t * ct, (t + 1) * ct)
        m = jnp.max(highest, axis=0, keepdims=True)
        if c > 0:
            m = jnp.maximum(m, m_old[t])
        highest, o = None, None
        for j in range(steps):
            if idx + 1 < len(items):
                highest = scores(idx + 1, j, highest)
            here = slice(j * sub, (j + 1) * sub)
            p = jnp.exp2(s_s[idx % 2, here, :] - m).astype(jnp.bfloat16)
            part = jnp.dot(vt_s[c % 2, :, here], p, preferred_element_type=jnp.float32)
            o = part if o is None else o + part
        if c > 0:
            o = o + jnp.exp2(m_old[t] - m) * acc_s[:, cols]
        acc_s[:, cols] = o
        m_old[t] = m
    total = acc_s[hd : hd + 1, :]
    out = (acc_s[:hd, :] / total).T.astype(jnp.bfloat16)
    m_all = jnp.concatenate([m_old[t] for t in range(tiles)], axis=1)
    lse = jnp.broadcast_to(m_all + jnp.log2(total), (hd, count)).T
    lane = lax.broadcasted_iota(jnp.int32, (slots, hd), 1)
    pieces = jnp.zeros((slots, hd), jnp.float32)
    for h in range(heads):
        out_ref[:, h * hd : (h + 1) * hd] = out[h * slots : (h + 1) * slots, :]
        rest = lse[h * slots : (h + 1) * slots, :]
        for j in range(3):
            part = rest.astype(jnp.bfloat16).astype(jnp.float32)
            rest = rest - part
            pieces = jnp.where(lane == j * heads + h, part, pieces)
    out_ref[:, feat:] = pieces.astype(jnp.bfloat16)


def combine_kernel(fork_ref, slot_ref, recv_ref, *refs, capacity, heads):
    out_ref = refs[-1]
    parts = [refs[i : i + 2] for i in range(0, len(refs) - 1, 2)]
    copies, rows, feat = out_ref.shape
    hd = feat // heads
    some = rows // len(parts)
    hot = half_slots(one_hot_slots(fork_ref, slot_ref, capacity), capacity)
    for half in range(2):
        got = jnp.dot(
            hot[half].T.astype(jnp.bfloat16), recv_ref[...], preferred_element_type=jnp.float32
        )
        for i in range(heads // 2):
            h = half * (heads // 2) + i
            cols = slice(h * hd, (h + 1) * hd)
            lse_pre = sum(
                got[:, feat // 2 + j * heads // 2 + i : feat // 2 + j * heads // 2 + i + 1]
                for j in range(3)
            )
            lse_pre = jnp.broadcast_to(lse_pre, (rows, hd))
            lse_suf = jnp.concatenate(
                [ref[pl.ds(h, some, stride=heads), :] for _, ref in parts], axis=0
            )
            o_suf = jnp.concatenate([ref[:, cols] for ref, _ in parts], axis=0)
            top = jnp.maximum(lse_pre, lse_suf)
            a = jnp.exp2(lse_pre - top)
            b = jnp.exp2(lse_suf - top)
            value = (a * got[:, i * hd : (i + 1) * hd] + b * o_suf) / (a + b)
            value = value.astype(jnp.bfloat16)
            for copy in range(copies):
                out_ref[copy, :, cols] = value


def body(queries, prefix_cache, suffix_cache, suffix_len, fork_prefix, prefix_slot, out_weight):
    rows, feat = queries.shape
    keys = prefix_cache.shape[1]
    hd = prefix_cache.shape[3] // 2
    heads = feat // hd
    owners = lax.axis_size("owner")
    prefixes = prefix_slot.shape[0]
    capacity = max(2, 2 * rows // prefixes)
    slots = prefixes * capacity
    scale = hd**-0.5
    fork_row = fork_prefix.reshape(1, rows)
    slot_row = prefix_slot.reshape(1, prefixes)

    def limit(mib):
        return pltpu.CompilerParams(vmem_limit_bytes=mib * MIB)

    places = slots * 2
    outgoing = pl.pallas_call(
        functools.partial(route_kernel, capacity=capacity),
        out_shape=jax.ShapeDtypeStruct((places, feat // 2), jnp.bfloat16),
        in_specs=[VMEM, VMEM, VMEM],
        out_specs=VMEM,
        name="route",
    )(fork_row, slot_row, queries)
    received = lax.all_to_all(
        outgoing.reshape(owners, places // owners, feat // 2),
        "owner",
        split_axis=0,
        concat_axis=0,
        tiled=True,
    )

    suffix_keys = suffix_cache.shape[1]
    some = rows // 2

    def suffix(first):
        return pl.pallas_call(
            functools.partial(suffix_kernel, first=first, group=GROUP_ROWS, scale=scale),
            out_shape=(
                jax.ShapeDtypeStruct((some, feat), jnp.float32),
                jax.ShapeDtypeStruct((some * heads, hd), jnp.float32),
            ),
            in_specs=[SMEM, VMEM, ANY],
            out_specs=(VMEM, VMEM),
            scratch_shapes=[
                pltpu.VMEM((some, suffix_keys, 2 * hd), jnp.bfloat16),
                pltpu.SemaphoreType.DMA((some,)),
                pltpu.VMEM((some * heads, hd), jnp.float32),
                pltpu.VMEM((some * heads, hd), jnp.float32),
            ],
            compiler_params=limit(44),
            cost_estimate=pl.CostEstimate(
                flops=4 * some * heads * suffix_keys * hd,
                bytes_accessed=some * suffix_keys * 4 * hd,
                transcendentals=some * heads * suffix_keys,
            ),
            name="suffix",
        )(suffix_len, queries, suffix_cache.reshape(rows, suffix_keys, 2 * hd))

    suffix_one = suffix(0)

    kb, ct, sub = 2048, 256, 512
    count = slots * heads
    partial = pl.pallas_call(
        functools.partial(prefix_kernel, kb=kb, ct=ct, sub=sub, scale=scale),
        out_shape=jax.ShapeDtypeStruct((places, feat // 2 + hd), jnp.bfloat16),
        in_specs=[VMEM, VMEM, ANY],
        out_specs=VMEM,
        scratch_shapes=[
            pltpu.VMEM((2 * hd, count), jnp.bfloat16),
            pltpu.VMEM((2, kb, ct), jnp.float32),
            pltpu.VMEM((hd + 16, count), jnp.float32),
            pltpu.VMEM((2, hd + 16, kb), jnp.bfloat16),
        ],
        compiler_params=limit(24),
        cost_estimate=pl.CostEstimate(
            flops=4 * count * keys * hd,
            bytes_accessed=keys * 4 * hd,
            transcendentals=count * keys,
        ),
        name="prefix",
    )(
        received.reshape(places, feat // 2),
        prefix_cache.reshape(keys, 2 * hd),
        suffix_one[1],
    )
    returned = lax.all_to_all(
        partial.reshape(owners, places // owners, feat // 2 + hd),
        "owner",
        split_axis=0,
        concat_axis=0,
        tiled=True,
    )
    suffix_two = suffix(some)

    attended = pl.pallas_call(
        functools.partial(combine_kernel, capacity=capacity, heads=heads),
        out_shape=jax.ShapeDtypeStruct((owners, rows, feat), jnp.bfloat16),
        in_specs=[VMEM] * 7,
        out_specs=VMEM,
        compiler_params=limit(8),
        name="combine",
    )(fork_row, slot_row, returned.reshape(places, feat // 2 + hd), *suffix_one, *suffix_two)
    gathered = lax.all_to_all(attended, "owner", split_axis=0, concat_axis=0, tiled=True)

    members = lax.axis_size("kv")
    chips = members // 2
    place = lax.axis_index("kv")
    chip, core = place // 2, place % 2
    block = owners * rows // members
    cols = out_weight.shape[1]
    full = gathered.reshape(chips, 2, block, feat)
    theirs = jnp.dot(
        lax.dynamic_index_in_dim(full, 1 - core, 1, keepdims=False).reshape(chips * block, feat),
        out_weight,
        preferred_element_type=jnp.float32,
    ).astype(jnp.bfloat16)
    from_pair = lax.ppermute(theirs, "kv", [(i, i ^ 1) for i in range(members)])
    mine = jnp.dot(
        lax.dynamic_index_in_dim(full, core, 1, keepdims=False).reshape(chips * block, feat),
        out_weight,
        preferred_element_type=jnp.float32,
    )
    pair_sum = (mine + from_pair.astype(jnp.float32)).reshape(chips, block, cols)
    pair_sent = pair_sum.astype(jnp.bfloat16)
    total = lax.dynamic_index_in_dim(pair_sum, chip, 0, keepdims=False)
    for d in range(1, chips):
        piece = lax.dynamic_index_in_dim(pair_sent, (chip + d) % chips, 0, keepdims=False)
        moved = lax.ppermute(
            piece,
            "kv",
            [(x * 2 + c, ((x + d) % chips) * 2 + c) for x in range(chips) for c in range(2)],
        )
        total = total + moved.astype(jnp.float32)
    return total.astype(jnp.bfloat16)


def solution(mesh):
    placed = (
        P("owner", "kv"),
        P("owner", None, "kv", None),
        P("owner", None, "kv", None),
        P("owner"),
        P("owner", None),
        P(),
        P("kv", "owner"),
    )
    return jax.shard_map(
        body, mesh=mesh, in_specs=placed, out_specs=P("kv", "owner"), check_vma=False
    )
```

```python
import functools

import jax
import jax.numpy as jnp
from jax import lax
from jax.experimental import pallas as pl
from jax.experimental.pallas import tpu as pltpu
from jax.sharding import PartitionSpec as P

LOG2E = 1.4426950408889634
NT = (((1,), (1,)), ((), ()))
VMEM = pl.BlockSpec(memory_space=pltpu.VMEM)
SMEM = pl.BlockSpec(memory_space=pltpu.SMEM)
ANY = pl.BlockSpec(memory_space=pl.ANY)
MIB = 2**20
GROUP_ROWS = 4


def one_hot_slots(ints_ref, rows, prefixes, capacity):
    sub = lax.broadcasted_iota(jnp.int32, (rows, rows), 0)
    lane = lax.broadcasted_iota(jnp.int32, (rows, rows), 1)
    eye = sub == lane
    fork_row = jnp.broadcast_to(ints_ref[:, :rows], (rows, rows))
    fork_col = jnp.sum(jnp.where(eye, fork_row, 0), axis=1, keepdims=True)
    picked = fork_col == lax.broadcasted_iota(jnp.int32, (rows, prefixes), 1)
    slots_all = jnp.broadcast_to(ints_ref[:, rows : rows + prefixes], (rows, prefixes))
    stored_col = jnp.sum(jnp.where(picked, slots_all, 0), axis=1, keepdims=True)
    stored_row = jnp.sum(
        jnp.where(eye, jnp.broadcast_to(stored_col, (rows, rows)), 0), axis=0, keepdims=True
    )
    earlier = (stored_col == stored_row) & (sub < lane)
    rank_row = jnp.sum(earlier.astype(jnp.int32), axis=0, keepdims=True)
    return stored_row, rank_row, prefixes


def half_slots(placed, capacity):
    stored_row, rank_row, prefixes = placed
    rows = stored_row.shape[1]
    place = lax.broadcasted_iota(jnp.int32, (prefixes * 2 * capacity, rows), 0)
    return [
        (place == (stored_row * 2 + half) * capacity + rank_row).astype(jnp.float32)
        for half in range(2)
    ]


def route_kernel(ints_ref, query_ref, out_ref, query_out, *, prefixes, capacity):
    query_out[...] = query_ref[...]
    rows, feat = query_ref.shape
    hot = half_slots(one_hot_slots(ints_ref, rows, prefixes, capacity), capacity)
    for half in range(2):
        cols = slice(half * feat // 2, (half + 1) * feat // 2)
        part = jnp.dot(
            hot[half].astype(jnp.bfloat16), query_ref[:, cols], preferred_element_type=jnp.float32
        )
        if half == 0:
            total = part
        else:
            total = total + part
    out_ref[...] = total.astype(jnp.bfloat16)


def suffix_kernel(
    len_hbm,
    q_hbm,
    kv_hbm,
    out_ref,
    lse_ref,
    kv,
    sems,
    lens,
    q,
    q_s,
    o_s,
    sem_l,
    sem_q,
    *,
    first,
    skip,
    group,
    scale,
):
    rows, keys, width = kv.shape
    hd = width // 2
    heads = q.shape[1] // hd
    c2 = scale * LOG2E
    span = group * heads
    groups = rows // group

    def rows_copy(r):
        return pltpu.make_async_copy(kv_hbm.at[first + r], kv.at[r], sems.at[r])

    copy_l = pltpu.make_async_copy(len_hbm, lens, sem_l)
    copy_q = pltpu.make_async_copy(q_hbm, q, sem_q)
    copy_l.start()
    copy_q.start()
    for r in range(rows):
        rows_copy(r).start()
    copy_q.wait()
    for h in range(heads):
        q_s[pl.ds(h, rows, stride=heads), :] = q[
            first : first + rows, h * hd : (h + 1) * hd
        ].astype(jnp.float32)
    copy_l.wait()
    row_id = lax.broadcasted_iota(jnp.int32, (span, 1), 0) // heads
    position = lax.broadcasted_iota(jnp.int32, (span, keys), 1)

    def scores(g):
        return jnp.concatenate(
            [
                lax.dot_general(
                    q_s[r * heads : (r + 1) * heads, :].astype(jnp.bfloat16),
                    kv[r, :, :hd],
                    NT,
                    preferred_element_type=jnp.float32,
                )
                for r in range(g * group, (g + 1) * group)
            ],
            axis=0,
        )

    for r in range(group):
        rows_copy(r).wait()
    s_next = scores(0)
    for g in range(groups):
        s = s_next
        if g + 1 < groups:
            for r in range((g + 1) * group, (g + 2) * group):
                rows_copy(r).wait()
            s_next = scores(g + 1)
        length = jnp.zeros((span, 1), jnp.int32)
        for i in range(group):
            length = jnp.where(row_id == i, lens[0, skip + first + g * group + i], length)
        s = jnp.where(position < length, s, -1e30)
        m = jnp.max(s, axis=-1, keepdims=True)
        p = jnp.exp2((s - m) * c2)
        total = jnp.sum(p, axis=-1, keepdims=True)
        o = jnp.concatenate(
            [
                jnp.dot(
                    p[i * heads : (i + 1) * heads].astype(jnp.bfloat16),
                    kv[g * group + i, :, hd:],
                    preferred_element_type=jnp.float32,
                )
                for i in range(group)
            ],
            axis=0,
        )
        o_s[g * span : (g + 1) * span, :] = o / total
        lse_ref[g * span : (g + 1) * span, :] = jnp.broadcast_to(
            m * c2 + jnp.log2(total), (span, hd)
        )
    for h in range(heads):
        out_ref[:, h * hd : (h + 1) * hd] = o_s[pl.ds(h, rows, stride=heads), :]


def prefix_kernel(
    x_ref, kv, after_ref, out_ref, q_s, s_s, acc_s, vt_s, *, kb, ct, sub, scale
):
    keys = kv.shape[0]
    hd = kv.shape[1] // 2
    slots, feat = x_ref.shape
    heads = feat // hd
    count = slots * heads
    c2 = scale * LOG2E
    qf = jnp.concatenate([x_ref[:, h * hd : (h + 1) * hd] for h in range(heads)], axis=0)
    qf = qf.astype(jnp.float32).T * c2
    hi = qf.astype(jnp.bfloat16)
    q_s[:hd, :] = hi
    q_s[hd:, :] = (qf - hi.astype(jnp.float32)).astype(jnp.bfloat16)
    vt_s[:, hd:, :] = jnp.ones((2, vt_s.shape[1] - hd, kb), jnp.bfloat16)
    tiles = count // ct
    steps = kb // sub
    items = [(c, t) for c in range(keys // kb) for t in range(tiles)]

    def scores(idx, j, highest):
        c, t = items[idx]
        here = slice(c * kb + j * sub, c * kb + (j + 1) * sub)
        k = kv[here, :hd]
        s = jnp.dot(
            jnp.concatenate([k, k], axis=1),
            q_s[:, t * ct : (t + 1) * ct],
            preferred_element_type=jnp.float32,
        )
        s_s[idx % 2, j * sub : (j + 1) * sub, :] = s
        if t == 0:
            vt_s[c % 2, :hd, j * sub : (j + 1) * sub] = kv[here, hd:].T
        top = jnp.max(s.reshape(sub // 8, 8, ct), axis=0)
        return top if highest is None else jnp.maximum(highest, top)

    highest = None
    for j in range(steps):
        highest = scores(0, j, highest)
    m_old = {}
    for idx, (c, t) in enumerate(items):
        cols = slice(t * ct, (t + 1) * ct)
        m = jnp.max(highest, axis=0, keepdims=True)
        if c > 0:
            m = jnp.maximum(m, m_old[t])
        highest, o = None, None
        for j in range(steps):
            if idx + 1 < len(items):
                highest = scores(idx + 1, j, highest)
            here = slice(j * sub, (j + 1) * sub)
            p = jnp.exp2(s_s[idx % 2, here, :] - m).astype(jnp.bfloat16)
            part = jnp.dot(vt_s[c % 2, :, here], p, preferred_element_type=jnp.float32)
            o = part if o is None else o + part
        if c > 0:
            o = o + jnp.exp2(m_old[t] - m) * acc_s[:, cols]
        acc_s[:, cols] = o
        m_old[t] = m
    total = acc_s[hd : hd + 1, :]
    out = (acc_s[:hd, :] / total).T.astype(jnp.bfloat16)
    m_all = jnp.concatenate([m_old[t] for t in range(tiles)], axis=1)
    lse = jnp.broadcast_to(m_all + jnp.log2(total), (hd, count)).T
    lane = lax.broadcasted_iota(jnp.int32, (slots, hd), 1)
    pieces = jnp.zeros((slots, hd), jnp.float32)
    for h in range(heads):
        out_ref[:, h * hd : (h + 1) * hd] = out[h * slots : (h + 1) * slots, :]
        rest = lse[h * slots : (h + 1) * slots, :]
        for j in range(3):
            part = rest.astype(jnp.bfloat16).astype(jnp.float32)
            rest = rest - part
            pieces = jnp.where(lane == j * heads + h, part, pieces)
    out_ref[:, feat:] = pieces.astype(jnp.bfloat16)


def combine_kernel(ints_ref, recv_ref, *refs, prefixes, capacity, heads):
    out_ref = refs[-1]
    parts = [refs[i : i + 2] for i in range(0, len(refs) - 1, 2)]
    rows, feat = out_ref.shape
    hd = feat // heads
    some = rows // len(parts)
    hot = half_slots(one_hot_slots(ints_ref, rows, prefixes, capacity), capacity)
    for half in range(2):
        got = jnp.dot(
            hot[half].T.astype(jnp.bfloat16), recv_ref[...], preferred_element_type=jnp.float32
        )
        for i in range(heads // 2):
            h = half * (heads // 2) + i
            cols = slice(h * hd, (h + 1) * hd)
            lse_pre = sum(
                got[:, feat // 2 + j * heads // 2 + i : feat // 2 + j * heads // 2 + i + 1]
                for j in range(3)
            )
            lse_pre = jnp.broadcast_to(lse_pre, (rows, hd))
            lse_suf = jnp.concatenate(
                [ref[pl.ds(h, some, stride=heads), :] for _, ref in parts], axis=0
            )
            o_suf = jnp.concatenate([ref[:, cols] for ref, _ in parts], axis=0)
            top = jnp.maximum(lse_pre, lse_suf)
            a = jnp.exp2(lse_pre - top)
            b = jnp.exp2(lse_suf - top)
            value = (a * got[:, i * hd : (i + 1) * hd] + b * o_suf) / (a + b)
            out_ref[:, cols] = value.astype(jnp.bfloat16)


def project_kernel(rows_ref, weight_ref, out_ref, *, other):
    chips, block, cols = out_ref.shape
    core = lax.rem(lax.axis_index("kv") + other, 2)
    left = jnp.concatenate(
        [
            rows_ref[pl.ds(pl.multiple_of((2 * x + core) * block, block), block), :]
            for x in range(chips)
        ],
        axis=0,
    )
    total = jnp.dot(left, weight_ref[...], preferred_element_type=jnp.float32)
    out_ref[...] = total.reshape(chips, block, cols).astype(out_ref.dtype)


def pair_kernel(mine_ref, other_ref, total_ref, *piece_refs):
    chips = mine_ref.shape[0]
    chip = lax.axis_index("kv") // 2
    total_ref[...] = mine_ref[chip] + other_ref[chip].astype(jnp.float32)
    for d, piece_ref in enumerate(piece_refs, 1):
        x = lax.rem(chip + d, chips)
        piece_ref[...] = (mine_ref[x] + other_ref[x].astype(jnp.float32)).astype(jnp.bfloat16)


def body(queries, prefix_cache, suffix_cache, suffix_len, fork_prefix, prefix_slot, out_weight):
    rows, feat = queries.shape
    keys = prefix_cache.shape[1]
    hd = prefix_cache.shape[3] // 2
    heads = feat // hd
    owners = lax.axis_size("owner")
    prefixes = prefix_slot.shape[0]
    capacity = max(2, 2 * rows // prefixes)
    slots = prefixes * capacity
    scale = hd**-0.5
    ints = jnp.concatenate([fork_prefix.reshape(rows), prefix_slot, suffix_len]).reshape(1, -1)

    def limit(mib):
        return pltpu.CompilerParams(vmem_limit_bytes=mib * MIB)

    places = slots * 2
    outgoing, queries_near = pl.pallas_call(
        functools.partial(route_kernel, prefixes=prefixes, capacity=capacity),
        out_shape=(
            jax.ShapeDtypeStruct((places, feat // 2), jnp.bfloat16),
            jax.ShapeDtypeStruct(queries.shape, queries.dtype),
        ),
        in_specs=[VMEM] * 2,
        out_specs=(VMEM,) * 2,
        compiler_params=limit(40),
        name="route",
    )(ints, queries)
    received = lax.all_to_all(
        outgoing.reshape(owners, places // owners, feat // 2),
        "owner",
        split_axis=0,
        concat_axis=0,
        tiled=True,
    )

    suffix_keys = suffix_cache.shape[1]
    some = rows // 2

    def suffix(first, room):
        return pl.pallas_call(
            functools.partial(suffix_kernel, first=first, skip=rows + prefixes, group=GROUP_ROWS, scale=scale),
            out_shape=(
                jax.ShapeDtypeStruct((some, feat), jnp.float32),
                jax.ShapeDtypeStruct((some * heads, hd), jnp.float32),
            ),
            in_specs=[ANY, ANY, ANY],
            out_specs=(VMEM, VMEM),
            scratch_shapes=[
                pltpu.VMEM((some, suffix_keys, 2 * hd), jnp.bfloat16),
                pltpu.SemaphoreType.DMA((some,)),
                pltpu.SMEM(ints.shape, jnp.int32),
                pltpu.VMEM(queries.shape, queries.dtype),
                pltpu.VMEM((some * heads, hd), jnp.float32),
                pltpu.VMEM((some * heads, hd), jnp.float32),
                pltpu.SemaphoreType.DMA,
                pltpu.SemaphoreType.DMA,
            ],
            compiler_params=limit(room),
            cost_estimate=pl.CostEstimate(
                flops=4 * some * heads * suffix_keys * hd,
                bytes_accessed=some * suffix_keys * 4 * hd,
                transcendentals=some * heads * suffix_keys,
            ),
            name="suffix",
        )(ints, queries_near, suffix_cache.reshape(rows, suffix_keys, 2 * hd))

    suffix_one = suffix(0, 44)

    kb, ct, sub = 2048, 512, 1024
    count = slots * heads
    partial = pl.pallas_call(
        functools.partial(prefix_kernel, kb=kb, ct=ct, sub=sub, scale=scale),
        out_shape=jax.ShapeDtypeStruct((places, feat // 2 + hd), jnp.bfloat16),
        in_specs=[VMEM, VMEM, ANY],
        out_specs=VMEM,
        scratch_shapes=[
            pltpu.VMEM((2 * hd, count), jnp.bfloat16),
            pltpu.VMEM((2, kb, ct), jnp.float32),
            pltpu.VMEM((hd + 16, count), jnp.float32),
            pltpu.VMEM((2, hd + 16, kb), jnp.bfloat16),
        ],
        compiler_params=limit(24),
        cost_estimate=pl.CostEstimate(
            flops=4 * count * keys * hd,
            bytes_accessed=keys * 4 * hd,
            transcendentals=count * keys,
        ),
        name="prefix",
    )(
        received.reshape(places, feat // 2),
        prefix_cache.reshape(keys, 2 * hd),
        suffix_one[1],
    )
    returned = lax.all_to_all(
        partial.reshape(owners, places // owners, feat // 2 + hd),
        "owner",
        split_axis=0,
        concat_axis=0,
        tiled=True,
    )
    suffix_two = suffix(some, 44)

    attended = pl.pallas_call(
        functools.partial(
            combine_kernel, prefixes=prefixes, capacity=capacity, heads=heads
        ),
        out_shape=jax.ShapeDtypeStruct((rows, feat), jnp.bfloat16),
        in_specs=[VMEM] * 6,
        out_specs=VMEM,
        compiler_params=limit(8),
        name="combine",
    )(ints, returned.reshape(places, feat // 2 + hd), *suffix_one, *suffix_two)
    copies = jnp.broadcast_to(attended[None], (owners, rows, feat))
    gathered = lax.all_to_all(copies, "owner", split_axis=0, concat_axis=0, tiled=True)

    members = lax.axis_size("kv")
    chips = members // 2
    block = owners * rows // members
    cols = out_weight.shape[1]
    gathered = gathered.reshape(owners * rows, feat)

    def project(other, dtype, name):
        return pl.pallas_call(
            functools.partial(project_kernel, other=other),
            out_shape=jax.ShapeDtypeStruct((chips, block, cols), dtype),
            in_specs=[VMEM, VMEM],
            out_specs=VMEM,
            compiler_params=limit(12),
            name=name,
        )(gathered, out_weight)

    theirs = project(1, jnp.bfloat16, "project_theirs")
    from_pair = lax.ppermute(theirs, "kv", [(i, i ^ 1) for i in range(members)])
    mine = project(0, jnp.float32, "project_mine")
    total, *pieces = pl.pallas_call(
        pair_kernel,
        out_shape=(
            jax.ShapeDtypeStruct((block, cols), jnp.float32),
            *[jax.ShapeDtypeStruct((block, cols), jnp.bfloat16)] * (chips - 1),
        ),
        in_specs=[VMEM, VMEM],
        out_specs=(VMEM,) * chips,
        compiler_params=limit(8),
        name="pair",
    )(mine, from_pair)
    for d, piece in enumerate(pieces, 1):
        moved = lax.ppermute(
            piece,
            "kv",
            [(x * 2 + c, ((x + d) % chips) * 2 + c) for x in range(chips) for c in range(2)],
        )
        total = total + moved.astype(jnp.float32)
    return total.astype(jnp.bfloat16)


def solution(mesh):
    placed = (
        P("owner", "kv"),
        P("owner", None, "kv", None),
        P("owner", None, "kv", None),
        P("owner"),
        P("owner", None),
        P(),
        P("kv", "owner"),
    )
    return jax.shard_map(
        body, mesh=mesh, in_specs=placed, out_specs=P("kv", "owner"), check_vma=False
    )
```

```python
import functools

import jax
import jax.numpy as jnp
from jax import lax
from jax.experimental import pallas as pl
from jax.experimental.pallas import tpu as pltpu
from jax.sharding import PartitionSpec as P

LOG2E = 1.4426950408889634
NT = (((1,), (1,)), ((), ()))
VMEM = pl.BlockSpec(memory_space=pltpu.VMEM)
SMEM = pl.BlockSpec(memory_space=pltpu.SMEM)
ANY = pl.BlockSpec(memory_space=pl.ANY)
MIB = 2**20
GROUP_ROWS = 4
PREFIX_MIB = 52


def one_hot_slots(ints_ref, rows, prefixes, capacity):
    sub = lax.broadcasted_iota(jnp.int32, (rows, rows), 0)
    lane = lax.broadcasted_iota(jnp.int32, (rows, rows), 1)
    eye = sub == lane
    fork_row = jnp.broadcast_to(ints_ref[:, :rows], (rows, rows))
    fork_col = jnp.sum(jnp.where(eye, fork_row, 0), axis=1, keepdims=True)
    picked = fork_col == lax.broadcasted_iota(jnp.int32, (rows, prefixes), 1)
    slots_all = jnp.broadcast_to(ints_ref[:, rows : rows + prefixes], (rows, prefixes))
    stored_col = jnp.sum(jnp.where(picked, slots_all, 0), axis=1, keepdims=True)
    stored_row = jnp.sum(
        jnp.where(eye, jnp.broadcast_to(stored_col, (rows, rows)), 0), axis=0, keepdims=True
    )
    earlier = (stored_col == stored_row) & (sub < lane)
    rank_row = jnp.sum(earlier.astype(jnp.int32), axis=0, keepdims=True)
    return stored_row, rank_row, prefixes


def half_slots(placed, capacity):
    stored_row, rank_row, prefixes = placed
    rows = stored_row.shape[1]
    place = lax.broadcasted_iota(jnp.int32, (prefixes * 2 * capacity, rows), 0)
    return [
        (place == (stored_row * 2 + half) * capacity + rank_row).astype(jnp.float32)
        for half in range(2)
    ]


def route_kernel(ints_ref, query_ref, out_ref, query_out, *, prefixes, capacity):
    query_out[...] = query_ref[...]
    rows, feat = query_ref.shape
    hot = half_slots(one_hot_slots(ints_ref, rows, prefixes, capacity), capacity)
    for half in range(2):
        cols = slice(half * feat // 2, (half + 1) * feat // 2)
        part = jnp.dot(
            hot[half].astype(jnp.bfloat16), query_ref[:, cols], preferred_element_type=jnp.float32
        )
        if half == 0:
            total = part
        else:
            total = total + part
    out_ref[...] = total.astype(jnp.bfloat16)


def suffix_kernel(
    len_hbm,
    q_hbm,
    kv_hbm,
    out_ref,
    lse_ref,
    kv,
    sems,
    lens,
    q,
    q_s,
    o_s,
    sem_l,
    sem_q,
    *,
    first,
    skip,
    group,
    scale,
):
    rows, keys, width = kv.shape
    hd = width // 2
    heads = q.shape[1] // hd
    c2 = scale * LOG2E
    span = group * heads
    groups = rows // group

    def rows_copy(r):
        return pltpu.make_async_copy(kv_hbm.at[first + r], kv.at[r], sems.at[r])

    copy_l = pltpu.make_async_copy(len_hbm, lens, sem_l)
    copy_q = pltpu.make_async_copy(q_hbm, q, sem_q)
    copy_l.start()
    copy_q.start()
    for r in range(rows):
        rows_copy(r).start()
    copy_q.wait()
    for h in range(heads):
        q_s[pl.ds(h, rows, stride=heads), :] = q[
            first : first + rows, h * hd : (h + 1) * hd
        ].astype(jnp.float32)
    copy_l.wait()
    row_id = lax.broadcasted_iota(jnp.int32, (span, 1), 0) // heads
    position = lax.broadcasted_iota(jnp.int32, (span, keys), 1)

    def scores(g):
        return jnp.concatenate(
            [
                lax.dot_general(
                    q_s[r * heads : (r + 1) * heads, :].astype(jnp.bfloat16),
                    kv[r, :, :hd],
                    NT,
                    preferred_element_type=jnp.float32,
                )
                for r in range(g * group, (g + 1) * group)
            ],
            axis=0,
        )

    for r in range(group):
        rows_copy(r).wait()
    s_next = scores(0)
    for g in range(groups):
        s = s_next
        if g + 1 < groups:
            for r in range((g + 1) * group, (g + 2) * group):
                rows_copy(r).wait()
            s_next = scores(g + 1)
        length = jnp.zeros((span, 1), jnp.int32)
        for i in range(group):
            length = jnp.where(row_id == i, lens[0, skip + first + g * group + i], length)
        s = jnp.where(position < length, s, -1e30)
        m = jnp.max(s, axis=-1, keepdims=True)
        p = jnp.exp2((s - m) * c2)
        total = jnp.sum(p, axis=-1, keepdims=True)
        o = jnp.concatenate(
            [
                jnp.dot(
                    p[i * heads : (i + 1) * heads].astype(jnp.bfloat16),
                    kv[g * group + i, :, hd:],
                    preferred_element_type=jnp.float32,
                )
                for i in range(group)
            ],
            axis=0,
        )
        o_s[g * span : (g + 1) * span, :] = o / total
        lse_ref[g * span : (g + 1) * span, :] = jnp.broadcast_to(
            m * c2 + jnp.log2(total), (span, hd)
        )
    for h in range(heads):
        out_ref[:, h * hd : (h + 1) * hd] = o_s[pl.ds(h, rows, stride=heads), :]


def prefix_kernel(
    x_ref, kv_hbm, after_ref, out_ref, kv, sems, q_s, s_s, acc_s, vt_s, *, kb, ct, sub, scale
):
    keys = kv.shape[0]
    hd = kv.shape[1] // 2
    slots, feat = x_ref.shape
    heads = feat // hd
    count = slots * heads
    c2 = scale * LOG2E

    def copy_of(c):
        part = pl.ds(c * kb, kb)
        return pltpu.make_async_copy(kv_hbm.at[part], kv.at[part], sems.at[c])

    for c in range(keys // kb):
        copy_of(c).start()
    qf = jnp.concatenate([x_ref[:, h * hd : (h + 1) * hd] for h in range(heads)], axis=0)
    qf = qf.astype(jnp.float32).T * c2
    hi = qf.astype(jnp.bfloat16)
    q_s[:hd, :] = hi
    q_s[hd:, :] = (qf - hi.astype(jnp.float32)).astype(jnp.bfloat16)
    vt_s[:, hd:, :] = jnp.ones((2, vt_s.shape[1] - hd, kb), jnp.bfloat16)
    tiles = count // ct
    steps = kb // sub
    items = [(c, t) for c in range(keys // kb) for t in range(tiles)]

    def scores(idx, j, highest):
        c, t = items[idx]
        if j == 0 and t == 0:
            copy_of(c).wait()
        here = slice(c * kb + j * sub, c * kb + (j + 1) * sub)
        k = kv[here, :hd]
        s = jnp.dot(
            jnp.concatenate([k, k], axis=1),
            q_s[:, t * ct : (t + 1) * ct],
            preferred_element_type=jnp.float32,
        )
        s_s[idx % 2, j * sub : (j + 1) * sub, :] = s
        if t == 0:
            vt_s[c % 2, :hd, j * sub : (j + 1) * sub] = kv[here, hd:].T
        top = jnp.max(s.reshape(sub // 8, 8, ct), axis=0)
        return top if highest is None else jnp.maximum(highest, top)

    highest = None
    for j in range(steps):
        highest = scores(0, j, highest)
    m_old = {}
    for idx, (c, t) in enumerate(items):
        cols = slice(t * ct, (t + 1) * ct)
        m = jnp.max(highest, axis=0, keepdims=True)
        if c > 0:
            m = jnp.maximum(m, m_old[t])
        highest, o = None, None
        for j in range(steps):
            if idx + 1 < len(items):
                highest = scores(idx + 1, j, highest)
            here = slice(j * sub, (j + 1) * sub)
            p = jnp.exp2(s_s[idx % 2, here, :] - m).astype(jnp.bfloat16)
            part = jnp.dot(vt_s[c % 2, :, here], p, preferred_element_type=jnp.float32)
            o = part if o is None else o + part
        if c > 0:
            o = o + jnp.exp2(m_old[t] - m) * acc_s[:, cols]
        acc_s[:, cols] = o
        m_old[t] = m
    total = acc_s[hd : hd + 1, :]
    out = (acc_s[:hd, :] / total).T.astype(jnp.bfloat16)
    m_all = jnp.concatenate([m_old[t] for t in range(tiles)], axis=1)
    lse = jnp.broadcast_to(m_all + jnp.log2(total), (hd, count)).T
    lane = lax.broadcasted_iota(jnp.int32, (slots, hd), 1)
    pieces = jnp.zeros((slots, hd), jnp.float32)
    for h in range(heads):
        out_ref[:, h * hd : (h + 1) * hd] = out[h * slots : (h + 1) * slots, :]
        rest = lse[h * slots : (h + 1) * slots, :]
        for j in range(3):
            part = rest.astype(jnp.bfloat16).astype(jnp.float32)
            rest = rest - part
            pieces = jnp.where(lane == j * heads + h, part, pieces)
    out_ref[:, feat:] = pieces.astype(jnp.bfloat16)


def combine_kernel(ints_ref, recv_ref, *refs, prefixes, capacity, heads):
    out_ref = refs[-1]
    parts = [refs[i : i + 2] for i in range(0, len(refs) - 1, 2)]
    rows, feat = out_ref.shape
    hd = feat // heads
    some = rows // len(parts)
    hot = half_slots(one_hot_slots(ints_ref, rows, prefixes, capacity), capacity)
    for half in range(2):
        got = jnp.dot(
            hot[half].T.astype(jnp.bfloat16), recv_ref[...], preferred_element_type=jnp.float32
        )
        for i in range(heads // 2):
            h = half * (heads // 2) + i
            cols = slice(h * hd, (h + 1) * hd)
            lse_pre = sum(
                got[:, feat // 2 + j * heads // 2 + i : feat // 2 + j * heads // 2 + i + 1]
                for j in range(3)
            )
            lse_pre = jnp.broadcast_to(lse_pre, (rows, hd))
            lse_suf = jnp.concatenate(
                [ref[pl.ds(h, some, stride=heads), :] for _, ref in parts], axis=0
            )
            o_suf = jnp.concatenate([ref[:, cols] for ref, _ in parts], axis=0)
            top = jnp.maximum(lse_pre, lse_suf)
            a = jnp.exp2(lse_pre - top)
            b = jnp.exp2(lse_suf - top)
            value = (a * got[:, i * hd : (i + 1) * hd] + b * o_suf) / (a + b)
            out_ref[:, cols] = value.astype(jnp.bfloat16)


def project_kernel(rows_ref, weight_ref, out_ref, *, other):
    chips, block, cols = out_ref.shape
    core = lax.rem(lax.axis_index("kv") + other, 2)
    left = jnp.concatenate(
        [
            rows_ref[pl.ds(pl.multiple_of((2 * x + core) * block, block), block), :]
            for x in range(chips)
        ],
        axis=0,
    )
    total = jnp.dot(left, weight_ref[...], preferred_element_type=jnp.float32)
    out_ref[...] = total.reshape(chips, block, cols).astype(out_ref.dtype)


def pair_kernel(mine_ref, other_ref, total_ref, *piece_refs):
    chips = mine_ref.shape[0]
    chip = lax.axis_index("kv") // 2
    total_ref[...] = mine_ref[chip] + other_ref[chip].astype(jnp.float32)
    for d, piece_ref in enumerate(piece_refs, 1):
        x = lax.rem(chip + d, chips)
        piece_ref[...] = (mine_ref[x] + other_ref[x].astype(jnp.float32)).astype(jnp.bfloat16)


def body(queries, prefix_cache, suffix_cache, suffix_len, fork_prefix, prefix_slot, out_weight):
    rows, feat = queries.shape
    keys = prefix_cache.shape[1]
    hd = prefix_cache.shape[3] // 2
    heads = feat // hd
    owners = lax.axis_size("owner")
    prefixes = prefix_slot.shape[0]
    capacity = max(2, 2 * rows // prefixes)
    slots = prefixes * capacity
    scale = hd**-0.5
    ints = jnp.concatenate([fork_prefix.reshape(rows), prefix_slot, suffix_len]).reshape(1, -1)

    def limit(mib):
        return pltpu.CompilerParams(vmem_limit_bytes=mib * MIB)

    places = slots * 2
    outgoing, queries_near = pl.pallas_call(
        functools.partial(route_kernel, prefixes=prefixes, capacity=capacity),
        out_shape=(
            jax.ShapeDtypeStruct((places, feat // 2), jnp.bfloat16),
            jax.ShapeDtypeStruct(queries.shape, queries.dtype),
        ),
        in_specs=[VMEM] * 2,
        out_specs=(VMEM,) * 2,
        compiler_params=limit(40),
        name="route",
    )(ints, queries)
    received = lax.all_to_all(
        outgoing.reshape(owners, places // owners, feat // 2),
        "owner",
        split_axis=0,
        concat_axis=0,
        tiled=True,
    )

    suffix_keys = suffix_cache.shape[1]
    some = rows // 2

    def suffix(first, room):
        return pl.pallas_call(
            functools.partial(suffix_kernel, first=first, skip=rows + prefixes, group=GROUP_ROWS, scale=scale),
            out_shape=(
                jax.ShapeDtypeStruct((some, feat), jnp.float32),
                jax.ShapeDtypeStruct((some * heads, hd), jnp.float32),
            ),
            in_specs=[ANY, ANY, ANY],
            out_specs=(VMEM, VMEM),
            scratch_shapes=[
                pltpu.VMEM((some, suffix_keys, 2 * hd), jnp.bfloat16),
                pltpu.SemaphoreType.DMA((some,)),
                pltpu.SMEM(ints.shape, jnp.int32),
                pltpu.VMEM(queries.shape, queries.dtype),
                pltpu.VMEM((some * heads, hd), jnp.float32),
                pltpu.VMEM((some * heads, hd), jnp.float32),
                pltpu.SemaphoreType.DMA,
                pltpu.SemaphoreType.DMA,
            ],
            compiler_params=limit(room),
            cost_estimate=pl.CostEstimate(
                flops=4 * some * heads * suffix_keys * hd,
                bytes_accessed=some * suffix_keys * 4 * hd,
                transcendentals=some * heads * suffix_keys,
            ),
            name="suffix",
        )(ints, queries_near, suffix_cache.reshape(rows, suffix_keys, 2 * hd))

    suffix_one = suffix(0, 44)

    kb, ct, sub = 1024, 512, 1024
    count = slots * heads
    partial = pl.pallas_call(
        functools.partial(prefix_kernel, kb=kb, ct=ct, sub=sub, scale=scale),
        out_shape=jax.ShapeDtypeStruct((places, feat // 2 + hd), jnp.bfloat16),
        in_specs=[VMEM, ANY, ANY],
        out_specs=VMEM,
        scratch_shapes=[
            pltpu.VMEM((keys, 2 * hd), jnp.bfloat16),
            pltpu.SemaphoreType.DMA((keys // kb,)),
            pltpu.VMEM((2 * hd, count), jnp.bfloat16),
            pltpu.VMEM((2, kb, ct), jnp.float32),
            pltpu.VMEM((hd + 16, count), jnp.float32),
            pltpu.VMEM((2, hd + 16, kb), jnp.bfloat16),
        ],
        compiler_params=limit(PREFIX_MIB),
        cost_estimate=pl.CostEstimate(
            flops=4 * count * keys * hd,
            bytes_accessed=keys * 4 * hd,
            transcendentals=count * keys,
        ),
        name="prefix",
    )(
        received.reshape(places, feat // 2),
        prefix_cache.reshape(keys, 2 * hd),
        suffix_one[1],
    )
    returned = lax.all_to_all(
        partial.reshape(owners, places // owners, feat // 2 + hd),
        "owner",
        split_axis=0,
        concat_axis=0,
        tiled=True,
    )
    suffix_two = suffix(some, 44)

    attended = pl.pallas_call(
        functools.partial(
            combine_kernel, prefixes=prefixes, capacity=capacity, heads=heads
        ),
        out_shape=jax.ShapeDtypeStruct((rows, feat), jnp.bfloat16),
        in_specs=[VMEM] * 6,
        out_specs=VMEM,
        compiler_params=limit(8),
        name="combine",
    )(ints, returned.reshape(places, feat // 2 + hd), *suffix_one, *suffix_two)
    copies = jnp.broadcast_to(attended[None], (owners, rows, feat))
    gathered = lax.all_to_all(copies, "owner", split_axis=0, concat_axis=0, tiled=True)

    members = lax.axis_size("kv")
    chips = members // 2
    block = owners * rows // members
    cols = out_weight.shape[1]
    gathered = gathered.reshape(owners * rows, feat)

    def project(other, dtype, name):
        return pl.pallas_call(
            functools.partial(project_kernel, other=other),
            out_shape=jax.ShapeDtypeStruct((chips, block, cols), dtype),
            in_specs=[VMEM, VMEM],
            out_specs=VMEM,
            compiler_params=limit(12),
            name=name,
        )(gathered, out_weight)

    theirs = project(1, jnp.bfloat16, "project_theirs")
    from_pair = lax.ppermute(theirs, "kv", [(i, i ^ 1) for i in range(members)])
    mine = project(0, jnp.float32, "project_mine")
    total, *pieces = pl.pallas_call(
        pair_kernel,
        out_shape=(
            jax.ShapeDtypeStruct((block, cols), jnp.float32),
            *[jax.ShapeDtypeStruct((block, cols), jnp.bfloat16)] * (chips - 1),
        ),
        in_specs=[VMEM, VMEM],
        out_specs=(VMEM,) * chips,
        compiler_params=limit(8),
        name="pair",
    )(mine, from_pair)
    for d, piece in enumerate(pieces, 1):
        moved = lax.ppermute(
            piece,
            "kv",
            [(x * 2 + c, ((x + d) % chips) * 2 + c) for x in range(chips) for c in range(2)],
        )
        total = total + moved.astype(jnp.float32)
    return total.astype(jnp.bfloat16)


def solution(mesh):
    placed = (
        P("owner", "kv"),
        P("owner", None, "kv", None),
        P("owner", None, "kv", None),
        P("owner"),
        P("owner", None),
        P(),
        P("kv", "owner"),
    )
    return jax.shard_map(
        body, mesh=mesh, in_specs=placed, out_specs=P("kv", "owner"), check_vma=False
    )
```

```python
import functools

import jax
import jax.numpy as jnp
from jax import lax
from jax.experimental import pallas as pl
from jax.experimental.pallas import tpu as pltpu
from jax.sharding import PartitionSpec as P

LOG2E = 1.4426950408889634
NT = (((1,), (1,)), ((), ()))
VMEM = pl.BlockSpec(memory_space=pltpu.VMEM)
SMEM = pl.BlockSpec(memory_space=pltpu.SMEM)
ANY = pl.BlockSpec(memory_space=pl.ANY)
MIB = 2**20
GROUP_ROWS = 4
PREFIX_MIB = 52


def one_hot_slots(ints_ref, rows, prefixes, capacity):
    sub = lax.broadcasted_iota(jnp.int32, (rows, rows), 0)
    lane = lax.broadcasted_iota(jnp.int32, (rows, rows), 1)
    eye = sub == lane
    fork_row = jnp.broadcast_to(ints_ref[:, :rows], (rows, rows))
    fork_col = jnp.sum(jnp.where(eye, fork_row, 0), axis=1, keepdims=True)
    picked = fork_col == lax.broadcasted_iota(jnp.int32, (rows, prefixes), 1)
    slots_all = jnp.broadcast_to(ints_ref[:, rows : rows + prefixes], (rows, prefixes))
    stored_col = jnp.sum(jnp.where(picked, slots_all, 0), axis=1, keepdims=True)
    stored_row = jnp.sum(
        jnp.where(eye, jnp.broadcast_to(stored_col, (rows, rows)), 0), axis=0, keepdims=True
    )
    earlier = (stored_col == stored_row) & (sub < lane)
    rank_row = jnp.sum(earlier.astype(jnp.int32), axis=0, keepdims=True)
    return stored_row, rank_row, prefixes


def half_slots(placed, capacity):
    stored_row, rank_row, prefixes = placed
    rows = stored_row.shape[1]
    place = lax.broadcasted_iota(jnp.int32, (prefixes * 2 * capacity, rows), 0)
    return [
        (place == (stored_row * 2 + half) * capacity + rank_row).astype(jnp.float32)
        for half in range(2)
    ]


def route_kernel(ints_ref, query_ref, out_ref, query_out, *, prefixes, capacity):
    query_out[...] = query_ref[...]
    rows, feat = query_ref.shape
    hot = half_slots(one_hot_slots(ints_ref, rows, prefixes, capacity), capacity)
    for half in range(2):
        cols = slice(half * feat // 2, (half + 1) * feat // 2)
        part = jnp.dot(
            hot[half].astype(jnp.bfloat16), query_ref[:, cols], preferred_element_type=jnp.float32
        )
        if half == 0:
            total = part
        else:
            total = total + part
    out_ref[...] = total.astype(jnp.bfloat16)


def suffix_kernel(
    len_hbm,
    q_hbm,
    kv_hbm,
    out_ref,
    lse_ref,
    kv,
    sems,
    lens,
    q,
    q_s,
    o_s,
    sem_l,
    sem_q,
    *,
    first,
    skip,
    group,
    scale,
):
    rows, keys, width = kv.shape
    hd = width // 2
    heads = q.shape[1] // hd
    c2 = scale * LOG2E
    span = group * heads
    groups = rows // group

    def rows_copy(r):
        return pltpu.make_async_copy(kv_hbm.at[first + r], kv.at[r], sems.at[r])

    copy_l = pltpu.make_async_copy(len_hbm, lens, sem_l)
    copy_q = pltpu.make_async_copy(q_hbm, q, sem_q)
    copy_l.start()
    copy_q.start()
    for r in range(rows):
        rows_copy(r).start()
    copy_q.wait()
    for h in range(heads):
        q_s[pl.ds(h, rows, stride=heads), :] = q[
            first : first + rows, h * hd : (h + 1) * hd
        ].astype(jnp.float32)
    copy_l.wait()
    row_id = lax.broadcasted_iota(jnp.int32, (span, 1), 0) // heads
    position = lax.broadcasted_iota(jnp.int32, (span, keys), 1)

    def scores(g):
        return jnp.concatenate(
            [
                lax.dot_general(
                    q_s[r * heads : (r + 1) * heads, :].astype(jnp.bfloat16),
                    kv[r, :, :hd],
                    NT,
                    preferred_element_type=jnp.float32,
                )
                for r in range(g * group, (g + 1) * group)
            ],
            axis=0,
        )

    for r in range(group):
        rows_copy(r).wait()
    s_next = scores(0)
    for g in range(groups):
        s = s_next
        if g + 1 < groups:
            for r in range((g + 1) * group, (g + 2) * group):
                rows_copy(r).wait()
            s_next = scores(g + 1)
        length = jnp.zeros((span, 1), jnp.int32)
        for i in range(group):
            length = jnp.where(row_id == i, lens[0, skip + first + g * group + i], length)
        s = jnp.where(position < length, s, -1e30)
        m = jnp.max(s, axis=-1, keepdims=True)
        p = jnp.exp2((s - m) * c2)
        total = jnp.sum(p, axis=-1, keepdims=True)
        o = jnp.concatenate(
            [
                jnp.dot(
                    p[i * heads : (i + 1) * heads].astype(jnp.bfloat16),
                    kv[g * group + i, :, hd:],
                    preferred_element_type=jnp.float32,
                )
                for i in range(group)
            ],
            axis=0,
        )
        o_s[g * span : (g + 1) * span, :] = o / total
        lse_ref[g * span : (g + 1) * span, :] = jnp.broadcast_to(
            m * c2 + jnp.log2(total), (span, hd)
        )
    for h in range(heads):
        out_ref[:, h * hd : (h + 1) * hd] = o_s[pl.ds(h, rows, stride=heads), :]


def prefix_kernel(
    x_ref, kv_hbm, after_ref, out_ref, kv, sems, q_s, s_s, acc_s, vt_s, *, kb, ct, sub, scale
):
    keys = kv.shape[0]
    hd = kv.shape[1] // 2
    slots, feat = x_ref.shape
    heads = feat // hd
    count = slots * heads
    c2 = scale * LOG2E

    pieces_at, begin = {}, 0
    while begin < keys // kb:
        pieces_at[begin] = max(1, begin)
        begin += pieces_at[begin]

    def copy_of(c):
        part = pl.ds(c * kb, min(pieces_at[c], keys // kb - c) * kb)
        return pltpu.make_async_copy(kv_hbm.at[part], kv.at[part], sems.at[c])

    for c in pieces_at:
        copy_of(c).start()
    qf = jnp.concatenate([x_ref[:, h * hd : (h + 1) * hd] for h in range(heads)], axis=0)
    qf = qf.astype(jnp.float32).T * c2
    hi = qf.astype(jnp.bfloat16)
    q_s[:hd, :] = hi
    q_s[hd:, :] = (qf - hi.astype(jnp.float32)).astype(jnp.bfloat16)
    vt_s[:, hd:, :] = jnp.ones((2, vt_s.shape[1] - hd, kb), jnp.bfloat16)
    tiles = count // ct
    steps = kb // sub
    items = [(c, t) for c in range(keys // kb) for t in range(tiles)]

    def scores(idx, j, highest):
        c, t = items[idx]
        if j == 0 and t == 0 and c in pieces_at:
            copy_of(c).wait()
        here = slice(c * kb + j * sub, c * kb + (j + 1) * sub)
        k = kv[here, :hd]
        s = jnp.dot(
            jnp.concatenate([k, k], axis=1),
            q_s[:, t * ct : (t + 1) * ct],
            preferred_element_type=jnp.float32,
        )
        s_s[idx % 2, j * sub : (j + 1) * sub, :] = s
        if t == 0:
            vt_s[c % 2, :hd, j * sub : (j + 1) * sub] = kv[here, hd:].T
        top = jnp.max(s.reshape(sub // 8, 8, ct), axis=0)
        return top if highest is None else jnp.maximum(highest, top)

    highest = None
    for j in range(steps):
        highest = scores(0, j, highest)
    m_old = {}
    for idx, (c, t) in enumerate(items):
        cols = slice(t * ct, (t + 1) * ct)
        m = jnp.max(highest, axis=0, keepdims=True)
        if c > 0:
            m = jnp.maximum(m, m_old[t])
        highest, o = None, None
        for j in range(steps):
            if idx + 1 < len(items):
                highest = scores(idx + 1, j, highest)
            here = slice(j * sub, (j + 1) * sub)
            p = jnp.exp2(s_s[idx % 2, here, :] - m).astype(jnp.bfloat16)
            part = jnp.dot(vt_s[c % 2, :, here], p, preferred_element_type=jnp.float32)
            o = part if o is None else o + part
        if c > 0:
            o = o + jnp.exp2(m_old[t] - m) * acc_s[:, cols]
        acc_s[:, cols] = o
        m_old[t] = m
    total = acc_s[hd : hd + 1, :]
    out = (acc_s[:hd, :] / total).T.astype(jnp.bfloat16)
    m_all = jnp.concatenate([m_old[t] for t in range(tiles)], axis=1)
    lse = jnp.broadcast_to(m_all + jnp.log2(total), (hd, count)).T
    lane = lax.broadcasted_iota(jnp.int32, (slots, hd), 1)
    pieces = jnp.zeros((slots, hd), jnp.float32)
    for h in range(heads):
        out_ref[:, h * hd : (h + 1) * hd] = out[h * slots : (h + 1) * slots, :]
        rest = lse[h * slots : (h + 1) * slots, :]
        for j in range(3):
            part = rest.astype(jnp.bfloat16).astype(jnp.float32)
            rest = rest - part
            pieces = jnp.where(lane == j * heads + h, part, pieces)
    out_ref[:, feat:] = pieces.astype(jnp.bfloat16)


def combine_kernel(ints_ref, recv_ref, *refs, prefixes, capacity, heads):
    out_ref = refs[-1]
    parts = [refs[i : i + 2] for i in range(0, len(refs) - 1, 2)]
    rows, feat = out_ref.shape
    hd = feat // heads
    some = rows // len(parts)
    hot = half_slots(one_hot_slots(ints_ref, rows, prefixes, capacity), capacity)
    for half in range(2):
        got = jnp.dot(
            hot[half].T.astype(jnp.bfloat16), recv_ref[...], preferred_element_type=jnp.float32
        )
        for i in range(heads // 2):
            h = half * (heads // 2) + i
            cols = slice(h * hd, (h + 1) * hd)
            lse_pre = sum(
                got[:, feat // 2 + j * heads // 2 + i : feat // 2 + j * heads // 2 + i + 1]
                for j in range(3)
            )
            lse_pre = jnp.broadcast_to(lse_pre, (rows, hd))
            lse_suf = jnp.concatenate(
                [ref[pl.ds(h, some, stride=heads), :] for _, ref in parts], axis=0
            )
            o_suf = jnp.concatenate([ref[:, cols] for ref, _ in parts], axis=0)
            top = jnp.maximum(lse_pre, lse_suf)
            a = jnp.exp2(lse_pre - top)
            b = jnp.exp2(lse_suf - top)
            value = (a * got[:, i * hd : (i + 1) * hd] + b * o_suf) / (a + b)
            out_ref[:, cols] = value.astype(jnp.bfloat16)


def project_kernel(rows_ref, weight_ref, out_ref, *, other):
    chips, block, cols = out_ref.shape
    core = lax.rem(lax.axis_index("kv") + other, 2)
    left = jnp.concatenate(
        [
            rows_ref[pl.ds(pl.multiple_of((2 * x + core) * block, block), block), :]
            for x in range(chips)
        ],
        axis=0,
    )
    total = jnp.dot(left, weight_ref[...], preferred_element_type=jnp.float32)
    out_ref[...] = total.reshape(chips, block, cols).astype(out_ref.dtype)


def pair_kernel(mine_ref, other_ref, total_ref, *piece_refs):
    chips = mine_ref.shape[0]
    chip = lax.axis_index("kv") // 2
    total_ref[...] = mine_ref[chip] + other_ref[chip].astype(jnp.float32)
    for d, piece_ref in enumerate(piece_refs, 1):
        x = lax.rem(chip + d, chips)
        piece_ref[...] = (mine_ref[x] + other_ref[x].astype(jnp.float32)).astype(jnp.bfloat16)


def body(queries, prefix_cache, suffix_cache, suffix_len, fork_prefix, prefix_slot, out_weight):
    rows, feat = queries.shape
    keys = prefix_cache.shape[1]
    hd = prefix_cache.shape[3] // 2
    heads = feat // hd
    owners = lax.axis_size("owner")
    prefixes = prefix_slot.shape[0]
    capacity = max(2, 2 * rows // prefixes)
    slots = prefixes * capacity
    scale = hd**-0.5
    ints = jnp.concatenate([fork_prefix.reshape(rows), prefix_slot, suffix_len]).reshape(1, -1)

    def limit(mib):
        return pltpu.CompilerParams(vmem_limit_bytes=mib * MIB)

    places = slots * 2
    outgoing, queries_near = pl.pallas_call(
        functools.partial(route_kernel, prefixes=prefixes, capacity=capacity),
        out_shape=(
            jax.ShapeDtypeStruct((places, feat // 2), jnp.bfloat16),
            jax.ShapeDtypeStruct(queries.shape, queries.dtype),
        ),
        in_specs=[VMEM] * 2,
        out_specs=(VMEM,) * 2,
        compiler_params=limit(40),
        name="route",
    )(ints, queries)
    received = lax.all_to_all(
        outgoing.reshape(owners, places // owners, feat // 2),
        "owner",
        split_axis=0,
        concat_axis=0,
        tiled=True,
    )

    suffix_keys = suffix_cache.shape[1]
    some = rows // 2

    def suffix(first, room):
        return pl.pallas_call(
            functools.partial(suffix_kernel, first=first, skip=rows + prefixes, group=GROUP_ROWS, scale=scale),
            out_shape=(
                jax.ShapeDtypeStruct((some, feat), jnp.float32),
                jax.ShapeDtypeStruct((some * heads, hd), jnp.float32),
            ),
            in_specs=[ANY, ANY, ANY],
            out_specs=(VMEM, VMEM),
            scratch_shapes=[
                pltpu.VMEM((some, suffix_keys, 2 * hd), jnp.bfloat16),
                pltpu.SemaphoreType.DMA((some,)),
                pltpu.SMEM(ints.shape, jnp.int32),
                pltpu.VMEM(queries.shape, queries.dtype),
                pltpu.VMEM((some * heads, hd), jnp.float32),
                pltpu.VMEM((some * heads, hd), jnp.float32),
                pltpu.SemaphoreType.DMA,
                pltpu.SemaphoreType.DMA,
            ],
            compiler_params=limit(room),
            cost_estimate=pl.CostEstimate(
                flops=4 * some * heads * suffix_keys * hd,
                bytes_accessed=some * suffix_keys * 4 * hd,
                transcendentals=some * heads * suffix_keys,
            ),
            name="suffix",
        )(ints, queries_near, suffix_cache.reshape(rows, suffix_keys, 2 * hd))

    suffix_one = suffix(0, 44)

    kb, ct, sub = 1024, 512, 1024
    count = slots * heads
    partial = pl.pallas_call(
        functools.partial(prefix_kernel, kb=kb, ct=ct, sub=sub, scale=scale),
        out_shape=jax.ShapeDtypeStruct((places, feat // 2 + hd), jnp.bfloat16),
        in_specs=[VMEM, ANY, ANY],
        out_specs=VMEM,
        scratch_shapes=[
            pltpu.VMEM((keys, 2 * hd), jnp.bfloat16),
            pltpu.SemaphoreType.DMA((keys // kb,)),
            pltpu.VMEM((2 * hd, count), jnp.bfloat16),
            pltpu.VMEM((2, kb, ct), jnp.float32),
            pltpu.VMEM((hd + 16, count), jnp.float32),
            pltpu.VMEM((2, hd + 16, kb), jnp.bfloat16),
        ],
        compiler_params=limit(PREFIX_MIB),
        cost_estimate=pl.CostEstimate(
            flops=4 * count * keys * hd,
            bytes_accessed=keys * 4 * hd,
            transcendentals=count * keys,
        ),
        name="prefix",
    )(
        received.reshape(places, feat // 2),
        prefix_cache.reshape(keys, 2 * hd),
        suffix_one[1],
    )
    returned = lax.all_to_all(
        partial.reshape(owners, places // owners, feat // 2 + hd),
        "owner",
        split_axis=0,
        concat_axis=0,
        tiled=True,
    )
    suffix_two = suffix(some, 44)

    attended = pl.pallas_call(
        functools.partial(
            combine_kernel, prefixes=prefixes, capacity=capacity, heads=heads
        ),
        out_shape=jax.ShapeDtypeStruct((rows, feat), jnp.bfloat16),
        in_specs=[VMEM] * 6,
        out_specs=VMEM,
        compiler_params=limit(8),
        name="combine",
    )(ints, returned.reshape(places, feat // 2 + hd), *suffix_one, *suffix_two)
    copies = jnp.broadcast_to(attended[None], (owners, rows, feat))
    gathered = lax.all_to_all(copies, "owner", split_axis=0, concat_axis=0, tiled=True)

    members = lax.axis_size("kv")
    chips = members // 2
    block = owners * rows // members
    cols = out_weight.shape[1]
    gathered = gathered.reshape(owners * rows, feat)

    def project(other, dtype, name):
        return pl.pallas_call(
            functools.partial(project_kernel, other=other),
            out_shape=jax.ShapeDtypeStruct((chips, block, cols), dtype),
            in_specs=[VMEM, VMEM],
            out_specs=VMEM,
            compiler_params=limit(12),
            name=name,
        )(gathered, out_weight)

    theirs = project(1, jnp.bfloat16, "project_theirs")
    from_pair = lax.ppermute(theirs, "kv", [(i, i ^ 1) for i in range(members)])
    mine = project(0, jnp.float32, "project_mine")
    total, *pieces = pl.pallas_call(
        pair_kernel,
        out_shape=(
            jax.ShapeDtypeStruct((block, cols), jnp.float32),
            *[jax.ShapeDtypeStruct((block, cols), jnp.bfloat16)] * (chips - 1),
        ),
        in_specs=[VMEM, VMEM],
        out_specs=(VMEM,) * chips,
        compiler_params=limit(8),
        name="pair",
    )(mine, from_pair)
    for d, piece in enumerate(pieces, 1):
        moved = lax.ppermute(
            piece,
            "kv",
            [(x * 2 + c, ((x + d) % chips) * 2 + c) for x in range(chips) for c in range(2)],
        )
        total = total + moved.astype(jnp.float32)
    return total.astype(jnp.bfloat16)


def solution(mesh):
    placed = (
        P("owner", "kv"),
        P("owner", None, "kv", None),
        P("owner", None, "kv", None),
        P("owner"),
        P("owner", None),
        P(),
        P("kv", "owner"),
    )
    return jax.shard_map(
        body, mesh=mesh, in_specs=placed, out_specs=P("kv", "owner"), check_vma=False
    )
```
